32 devices in a mesh: rep: 8 (over y, x, core), fsdp: 4 (over z).
Axes of the slice: x: 2, y: 2, z: 4, core: 2. Of those that a mesh axis runs over, the one named last changes fastest.
Arguments:
- tokens: bfloat16 [16384, 1024], P(('rep', 'fsdp')), may hold values from -6 to 6
- cotangent: bfloat16 [16384, 1024], P(('rep', 'fsdp')), may hold values from -6 to 6
- valid_count: int32 [8, 4], P('rep', 'fsdp'), may hold values from 128 to 512, as said below
- norm_mix: bfloat16 [1024], P('fsdp'), may hold values from 0.5 to 1.5
- w_query: bfloat16 [1024, 1024], P('fsdp'), may hold values from -0.1875 to 0.1875
- w_key: bfloat16 [1024, 1024], P('fsdp'), may hold values from -0.1875 to 0.1875
- w_value: bfloat16 [1024, 2048], P('fsdp'), may hold values from -0.1875 to 0.1875
- w_gate: bfloat16 [1024, 2048], P('fsdp'), may hold values from -0.1875 to 0.1875
- w_beta: bfloat16 [1024, 8], P('fsdp'), may hold values from -0.1875 to 0.1875
- w_decay: bfloat16 [1024, 8], P('fsdp'), may hold values from -0.1875 to 0.1875
- a_log: float32 [8], replicated, may hold values from 0 to 2.77
- dt_bias: float32 [8], replicated, may hold values from -6.9 to -2.25
- conv_weight: bfloat16 [4, 4096], P(None, 'fsdp'), may hold values from -3 to 3
- norm_head: bfloat16 [256], P('fsdp'), may hold values from 0.5 to 1.5
- w_out: bfloat16 [2048, 1024], P('fsdp'), may hold values from -0.125 to 0.125
- norm_ffn: bfloat16 [1024], P('fsdp'), may hold values from 0.5 to 1.5
- w_ffgate: bfloat16 [1024, 2816], P(None, 'fsdp'), may hold values from -0.1875 to 0.1875
- w_ffup: bfloat16 [1024, 2816], P(None, 'fsdp'), may hold values from -0.1875 to 0.1875
- w_ffdown: bfloat16 [2816, 1024], P('fsdp'), may hold values from -0.109375 to 0.109375
Outputs:
- output: bfloat16 [16384, 1024], P(('rep', 'fsdp'))
- grad_tokens: float32 [16384, 1024], P(('rep', 'fsdp'))
- grad_norm_mix: float32 [1024], P('fsdp')
- grad_query: float32 [1024, 1024], P('fsdp')
- grad_key: float32 [1024, 1024], P('fsdp')
- grad_value: float32 [1024, 2048], P('fsdp')
- grad_gate: float32 [1024, 2048], P('fsdp')
- grad_beta: float32 [1024, 8], P('fsdp')
- grad_decay: float32 [1024, 8], P('fsdp')
- grad_a_log: float32 [8], replicated
- grad_dt_bias: float32 [8], replicated
- grad_conv: float32 [4, 4096], P(None, 'fsdp')
- grad_norm_head: float32 [256], P('fsdp')
- grad_out: float32 [2048, 1024], P('fsdp')
- grad_norm_ffn: float32 [1024], P('fsdp')
- grad_ffgate: float32 [1024, 2816], P(None, 'fsdp')
- grad_ffup: float32 [1024, 2816], P(None, 'fsdp')
- grad_ffdown: float32 [2816, 1024], P('fsdp')
The draws below stay inside these ranges and needn't reach their ends.
Inputs may be any that keep to these rules, and one draw needn't show every extreme that they name: Each device's rows below valid_count hold its part of its rep index's sequence; in every rep index one device has 512 valid rows and another has 128.
All inputs are finite; a program needn't handle non-finite values.
Results may differ from the reference program's by a relative error of at most 0.017.
Values may be sent and summed in bfloat16 or wider, within the bound.
No kernel may reach another device: no remote copies, remote signals or barrier semaphores. Data moves between devices by JAX's collectives and lax.ppermute only.
A program may use at most 384 MiB of HBM per device.

```python
import jax
import jax.numpy as jnp
from jax import lax

D = 1024
H = 8
DK = 128
DV = 256
FF = 2816
KW = 4
BLOCK = 64
SLOTS = 2048
TOK_DEV = 512
CONV = 4096
TOKENS = 16384
N_REP = 8
N_FSDP = 4


def draw_valid_count(key, part):
    key = jax.random.fold_in(key, 11)
    key_count, key_full, key_step = jax.random.split(key, 3)
    least_count = TOK_DEV // 4
    counts = jax.random.randint(key_count, (N_REP, N_FSDP), least_count, TOK_DEV + 1)
    full_place = jax.random.randint(key_full, (N_REP, 1), 0, N_FSDP)
    step_place = jax.random.randint(key_step, (N_REP, 1), 1, N_FSDP)
    least_place = (full_place + step_place) % N_FSDP
    columns = jnp.arange(N_FSDP)[None, :]
    counts = jnp.where(columns == full_place, TOK_DEV, counts)
    counts = jnp.where(columns == least_place, least_count, counts)
    return counts.astype(jnp.int32)


def shard_levels(rng, extent, cuts, low, top_value):
    def one(position, parts):
        steps = jax.random.uniform(jax.random.fold_in(jax.random.fold_in(rng, 6), position), (parts,), jnp.float32, low / len(cuts), top_value / len(cuts))
        return jnp.repeat(jnp.exp(steps), extent[position] // parts).reshape((-1,) + (1,) * (len(extent) - position - 1))

    level = one(*cuts[0])
    for cut in cuts[1:]:
        level = level * one(*cut)
    return level


def noise(key, dims, width, bound, cuts=(), held_as=jnp.bfloat16):
    loudness = shard_levels(key, dims, cuts, -0.22, 0.18) if cuts else 1.0
    values = jax.random.normal(key, dims, jnp.float32) * width * loudness
    return jnp.minimum(jnp.maximum(values, -bound), bound).astype(held_as)


def setup_inputs(seed: int = 0) -> dict:
    key_list = jax.random.split(jax.random.key(seed), 20)
    tokens = noise(key_list[0], (TOKENS, D), 1.0, 6.0, ((0, 32),))
    cotangent = noise(key_list[1], (TOKENS, D), 1.0, 6.0, ((0, 32),))
    valid_count = draw_valid_count(jax.random.fold_in(key_list[19], 71), 0)
    norm_mix = jnp.clip(1.0 + 0.1 * jax.random.normal(key_list[3], (D,), jnp.float32), 0.5, 1.5).astype(jnp.bfloat16)
    w_query = noise(key_list[4], (D, H * DK), D ** -0.5, 0.1875, ((0, 4),))
    w_key = noise(key_list[5], (D, H * DK), D ** -0.5, 0.1875, ((0, 4),))
    w_value = noise(key_list[6], (D, H * DV), D ** -0.5, 0.1875, ((0, 4),))
    w_gate = noise(key_list[7], (D, H * DV), D ** -0.5, 0.1875, ((0, 4),))
    w_beta = noise(key_list[8], (D, H), D ** -0.5, 0.1875, ((0, 4),))
    w_decay = noise(key_list[9], (D, H), D ** -0.5, 0.1875, ((0, 4),))
    a_log = jnp.clip(jax.random.uniform(key_list[10], (H,), jnp.float32, 0.0, 2.77), 0.0, 2.77)
    dt_bias = jnp.clip(jax.random.uniform(key_list[11], (H,), jnp.float32, -6.9, -2.25), -6.9, -2.25)
    conv_weight = noise(key_list[12], (KW, CONV), 0.5, 3.0, ((1, 4),))
    norm_head = jnp.clip(1.0 + 0.1 * jax.random.normal(key_list[13], (DV,), jnp.float32), 0.5, 1.5).astype(jnp.bfloat16)
    w_out = noise(key_list[14], (H * DV, D), (H * DV) ** -0.5, 0.125, ((0, 4),))
    norm_ffn = jnp.clip(1.0 + 0.1 * jax.random.normal(key_list[15], (D,), jnp.float32), 0.5, 1.5).astype(jnp.bfloat16)
    w_ffgate = noise(key_list[16], (D, FF), D ** -0.5, 0.1875, ((1, 4),))
    w_ffup = noise(key_list[17], (D, FF), D ** -0.5, 0.1875, ((1, 4),))
    w_ffdown = noise(key_list[18], (FF, D), FF ** -0.5, 0.109375, ((0, 4),))
    return dict(tokens=tokens, cotangent=cotangent, valid_count=valid_count, norm_mix=norm_mix, w_query=w_query, w_key=w_key, w_value=w_value, w_gate=w_gate, w_beta=w_beta, w_decay=w_decay, a_log=a_log, dt_bias=dt_bias, conv_weight=conv_weight, norm_head=norm_head, w_out=w_out, norm_ffn=norm_ffn, w_ffgate=w_ffgate, w_ffup=w_ffup, w_ffdown=w_ffdown)


norm_epsilon = 1e-06
head_epsilon = 1e-05
highest = lax.Precision.HIGHEST

@jax.custom_vjp
def low(v):
    return lax.optimization_barrier(v.astype(jnp.bfloat16)).astype(jnp.float32)

@jax.custom_vjp
def low_back(v):
    return v

def low_keep(v):
    return (low(v), None)

def low_pass(kept, grad):
    return (grad,)

def back_keep(v):
    return (v, None)

def back_low(kept, grad):
    return (low(grad),)
low.defvjp(low_keep, low_pass)
low_back.defvjp(back_keep, back_low)

def matmul_high(left, right):
    return jnp.dot(left, right, precision=highest)

def rms_scale(values, gain):
    return values * lax.rsqrt(lax.optimization_barrier(jnp.mean(values * values, -1, keepdims=True)) + norm_epsilon) * gain

def mixer_front(projected, previous, conv_full, beta_pre, decay_pre, a_log, dt_bias, valid_mask):
    row_count = projected.shape[0]
    head_count = a_log.shape[0]
    extended = jnp.concatenate([previous, projected], 0)
    convolved = conv_full[0] * extended[0:row_count]
    for j in range(1, KW):
        convolved = convolved + conv_full[j] * extended[j:j + row_count]
    activated = jax.nn.silu(convolved)
    qk_width = head_count * DK
    queries = activated[:, :qk_width].reshape(row_count, head_count, DK)
    key_vecs = activated[:, qk_width:2 * qk_width].reshape(row_count, head_count, DK)
    values = activated[:, 2 * qk_width:].reshape(row_count, head_count, DV)
    queries = queries * lax.rsqrt(lax.optimization_barrier(jnp.sum(queries * queries, -1, keepdims=True)) + norm_epsilon) * DK ** (-0.5)
    key_vecs = key_vecs * lax.rsqrt(lax.optimization_barrier(jnp.sum(key_vecs * key_vecs, -1, keepdims=True)) + norm_epsilon)
    beta_gate = valid_mask * jax.nn.sigmoid(beta_pre)
    log_decay = -valid_mask * jnp.exp(a_log) * jax.nn.softplus(decay_pre + dt_bias)
    return (queries, key_vecs, values, beta_gate, log_decay)

def to_blocks(values):
    row_count, head_count, inner = values.shape
    return values.reshape(row_count // BLOCK, BLOCK, head_count, inner).transpose(0, 2, 1, 3)

def to_heads(values):
    row_count, head_count = values.shape
    return values.reshape(row_count // BLOCK, BLOCK, head_count).transpose(0, 2, 1)

def block_parts(key_vecs, values, beta_gate, log_decay):
    keys_b = to_blocks(key_vecs)
    values_b = to_blocks(values)
    betas_b = to_heads(beta_gate)
    cum_log = jnp.cumsum(to_heads(log_decay), -1)
    places = jnp.arange(BLOCK)
    below_mask = places[:, None] > places[None, :]
    gap_log = cum_log[..., :, None] - cum_log[..., None, :]
    decay_mask = jnp.where(below_mask, jnp.exp(jnp.where(below_mask, gap_log, 0.0)), 0.0)
    key_inner = jnp.einsum('nhid,nhjd->nhij', keys_b, keys_b, precision=highest)
    system = jnp.eye(BLOCK, dtype=jnp.float32) + betas_b[..., :, None] * key_inner * decay_mask
    wy_keys = jax.scipy.linalg.solve_triangular(system, (betas_b * jnp.exp(cum_log))[..., None] * keys_b, lower=True, unit_diagonal=True)
    wy_values = jax.scipy.linalg.solve_triangular(system, betas_b[..., None] * values_b, lower=True, unit_diagonal=True)
    key_tilde = jnp.exp(cum_log[..., -1:] - cum_log)[..., None] * keys_b
    return (cum_log, wy_keys, wy_values, key_tilde)

def block_outputs(queries, key_vecs, cum_log, wy_keys, wy_values, key_tilde, start_state):
    row_count, head_count = (queries.shape[0], queries.shape[1])
    places = jnp.arange(BLOCK)
    within = places[:, None] >= places[None, :]

    def block_step(carried, pieces):
        query_b, key_b, cum_b, wkey_b, wval_b, ktil_b = pieces
        fresh_values = wval_b - jnp.einsum('hcd,hde->hce', wkey_b, carried, precision=highest)
        gap_log = cum_b[:, :, None] - cum_b[:, None, :]
        decay_mask = jnp.where(within, jnp.exp(jnp.where(within, gap_log, 0.0)), 0.0)
        scores = jnp.einsum('hid,hjd->hij', query_b, key_b, precision=highest) * decay_mask
        result = jnp.exp(cum_b)[..., None] * jnp.einsum('hcd,hde->hce', query_b, carried, precision=highest)
        result = result + jnp.einsum('hij,hje->hie', scores, fresh_values, precision=highest)
        next_state = jnp.exp(cum_b[:, -1])[:, None, None] * carried + jnp.einsum('hcd,hce->hde', ktil_b, fresh_values, precision=highest)
        return (next_state, result)
    final_state, results = lax.scan(jax.checkpoint(block_step), start_state, (to_blocks(queries), to_blocks(key_vecs), cum_log, wy_keys, wy_values, key_tilde))
    mixed_heads = results.transpose(0, 2, 1, 3).reshape(row_count, head_count * DV)
    return (mixed_heads, final_state)

def gate_tail(mixed_heads, gate_pre, head_gain):
    row_count = mixed_heads.shape[0]
    per_head = mixed_heads.reshape(row_count, -1, DV)
    scaled = per_head * lax.rsqrt(lax.optimization_barrier(jnp.mean(per_head * per_head, -1, keepdims=True)) + head_epsilon) * head_gain
    return scaled.reshape(row_count, -1) * jax.nn.silu(gate_pre)

def group_layer(inputs, counts, params):
    mix_gain, w_query, w_key, w_value, w_gate, w_beta, w_decay, a_log, dt_bias, conv_weight, head_gain, w_out, ffn_gain, w_ffgate, w_ffup, w_ffdown = params
    places = jnp.arange(TOK_DEV)
    valid_mask = (places[None, :] < counts[:, None]).astype(jnp.float32)[..., None]
    normed = low(rms_scale(inputs, mix_gain))
    projected = low_back(matmul_high(normed, jnp.concatenate([w_query, w_key, w_value], 1)))
    gate_pre = low_back(matmul_high(normed, w_gate))
    beta_pre = matmul_high(normed, w_beta)
    decay_pre = matmul_high(normed, w_decay)
    blocks = projected.reshape(N_FSDP, TOK_DEV, CONV)
    tail_rows = jax.vmap(lambda block_rows, valid_rows: lax.dynamic_slice_in_dim(block_rows, (valid_rows - (KW - 1)).astype(jnp.int32), KW - 1, 0))(blocks, counts)
    previous = jnp.concatenate([jnp.zeros((1, KW - 1, CONV), jnp.float32), tail_rows[:-1]], 0)
    fronts = jax.vmap(mixer_front, in_axes=(0, 0, None, 0, 0, None, None, 0))(blocks, previous, conv_weight, beta_pre.reshape(N_FSDP, TOK_DEV, H), decay_pre.reshape(N_FSDP, TOK_DEV, H), a_log, dt_bias, valid_mask)
    queries, key_vecs, values, beta_gate, log_decay = [member.reshape((SLOTS,) + member.shape[2:]) for member in fronts]
    cum_log, wy_keys, wy_values, key_tilde = block_parts(key_vecs, values, beta_gate, log_decay)
    mixed_heads, final_state = block_outputs(queries, key_vecs, cum_log, wy_keys, wy_values, key_tilde, jnp.zeros((H, DK, DV), jnp.float32))
    gated_out = low(gate_tail(mixed_heads, gate_pre, head_gain))
    residual = inputs + low_back(matmul_high(gated_out, w_out))
    normed_ffn = low(rms_scale(residual, ffn_gain))
    ff_gate = low_back(matmul_high(normed_ffn, w_ffgate))
    ff_up = low_back(matmul_high(normed_ffn, w_ffup))
    swiglu_out = low(jax.nn.silu(ff_gate) * ff_up)
    return (residual + low_back(matmul_high(swiglu_out, w_ffdown))) * valid_mask.reshape(SLOTS, 1)

def reference(tokens, cotangent, valid_count, norm_mix, w_query, w_key, w_value, w_gate, w_beta, w_decay, a_log, dt_bias, conv_weight, norm_head, w_out, norm_ffn, w_ffgate, w_ffup, w_ffdown):
    params = tuple((member.astype(jnp.float32) for member in (norm_mix, w_query, w_key, w_value, w_gate, w_beta, w_decay, a_log, dt_bias, conv_weight, norm_head, w_out, norm_ffn, w_ffgate, w_ffup, w_ffdown)))
    inputs = tokens.astype(jnp.float32)

    def forward(inputs, params):

        def one_group(pair):
            return group_layer(pair[0], pair[1], params)
        outputs = lax.map(jax.checkpoint(one_group), (inputs.reshape(N_REP, SLOTS, D), valid_count))
        return outputs.reshape(TOKENS, D)
    output, pull = jax.vjp(forward, inputs, params)
    grad_tokens, grads = pull(cotangent.astype(jnp.float32))
    return (output.astype(jnp.bfloat16), grad_tokens, grads[0], grads[1], grads[2], grads[3], grads[4], grads[5], grads[6], grads[7], grads[8], grads[9], grads[10], grads[11], grads[12], grads[13], grads[14], grads[15])
```

```python
import functools

import jax
import jax.numpy as jnp
from jax import lax
from jax.experimental import pallas as pl
from jax.experimental.pallas import tpu as pltpu
from jax.sharding import PartitionSpec as P

DK = 128
DV = 256
KW = 4
CHUNK = 128
PAD = 16
VMEM_LIMIT = 56 * 1024 * 1024

norm_epsilon = 1e-06
head_epsilon = 1e-05
highest = lax.Precision.HIGHEST
f32 = jnp.float32
bf16 = jnp.bfloat16


MM, MM_T, T_MM = ((1,), (0,)), ((1,), (1,)), ((0,), (0,))


def low_dot(a, b, dims):
    return lax.dot_general(a.astype(bf16), b.astype(bf16), (dims, ((), ())), preferred_element_type=f32)


def fine_dot(a, b, dims):
    a_high, b_high = a.astype(bf16), b.astype(bf16)
    a_low = (a - a_high.astype(f32)).astype(bf16)
    b_low = (b - b_high.astype(f32)).astype(bf16)
    return (
        low_dot(a_high, b_high, dims) + low_dot(a_high, b_low, dims) + low_dot(a_low, b_high, dims)
    )


def mm(a, b):
    return low_dot(a, b, MM)


def mm_t(a, b):
    return low_dot(a, b, MM_T)


def t_mm(a, b):
    return low_dot(a, b, T_MM)


def places():
    rows = lax.broadcasted_iota(jnp.int32, (CHUNK, CHUNK), 0)
    cols = lax.broadcasted_iota(jnp.int32, (CHUNK, CHUNK), 1)
    return rows, cols


def unit_lower_inverses(lows, rows, cols):
    differ = rows ^ cols
    eye = jnp.where(rows == cols, 1.0, 0.0)
    inverses = [eye - jnp.where(differ == 1, low, 0.0) for low in lows]
    size = 2
    while size < CHUNK:
        off = (differ >= size) & (differ < 2 * size)
        inner = [fine_dot(jnp.where(off, low, 0.0), inv, MM) for low, inv in zip(lows, inverses)]
        inverses = [inv - fine_dot(inv, part, MM) for inv, part in zip(inverses, inner)]
        size *= 2
    return inverses


def convolve(ext_ref, taps_ref, count):
    total = taps_ref[0:1, :] * ext_ref[PAD - KW + 1 : PAD - KW + 1 + count, :]
    for j in range(1, KW):
        start = PAD - KW + 1 + j
        total = total + taps_ref[j : j + 1, :] * ext_ref[start : start + count, :]
    return total


def sigmoid(z):
    return 1.0 / (1.0 + jnp.exp(-z))


def chunk_decay(col_ref, row_ref, part, rows, cols):
    beta = col_ref[0, part, 0:1]
    cum = col_ref[0, part, 1:2]
    gap = cum - row_ref[0, :, part]
    decay = jnp.where(rows >= cols, jnp.exp(jnp.minimum(gap, 0.0)), 0.0)
    last = cum[CHUNK - 1 : CHUNK, :]
    return beta, cum, decay, last


def front_kernel(
    xq, xk, xv, cq, ck, cv, col_ref, row_ref,
    q_out, k_out, inv_out, w_out, u_out, a_out, m_out, map_out, end_out,
):
    count = q_out.shape[0]
    rows, cols = places()
    eye = jnp.where(rows == cols, 1.0, 0.0)
    act = convolve(xq, cq, count)
    act = act * sigmoid(act)
    q_out[...] = act * lax.rsqrt(jnp.sum(act * act, -1, keepdims=True) + norm_epsilon) * DK ** (-0.5)
    act = convolve(xk, ck, count)
    act = act * sigmoid(act)
    k_out[...] = act * lax.rsqrt(jnp.sum(act * act, -1, keepdims=True) + norm_epsilon)
    act = convolve(xv, cv, count)
    values = act * sigmoid(act)
    blocks = range(count // CHUNK)
    parts = [slice(b * CHUNK, (b + 1) * CHUNK) for b in blocks]
    gates = [chunk_decay(col_ref, row_ref, part, rows, cols) for part in parts]
    keys = [k_out[part, :] for part in parts]
    lows = [
        beta * fine_dot(key, key, MM_T) * jnp.where(rows > cols, decay, 0.0)
        for key, (beta, _, decay, _) in zip(keys, gates)
    ]
    inverses = unit_lower_inverses(lows, rows, cols)
    steps, offsets = [], []
    for b, part, key, inverse, (beta, cum, decay, last) in zip(blocks, parts, keys, inverses, gates):
        inv_out[0, b] = inverse
        wkey = fine_dot(inverse, beta * jnp.exp(cum) * key, MM)
        wval = fine_dot(inverse, beta * values[part, :], MM)
        w_out[part, :] = wkey
        u_out[part, :] = wval
        a_out[0, b] = mm_t(q_out[part, :], key) * decay
        tilde = jnp.exp(last - cum) * key
        step = jnp.exp(last) * eye - t_mm(tilde, wkey)
        m_out[0, b] = step
        steps.append(step)
        offsets.append(t_mm(tilde, wval))
    transit, offset = eye, jnp.zeros((DK, DV), f32)
    for b in blocks:
        map_out[0, b, :, :DK] = transit
        map_out[0, b, :, DK:] = offset
        if b == 0:
            transit, offset = steps[0], offsets[0]
        else:
            transit, offset = fine_dot(steps[b], transit, MM), fine_dot(steps[b], offset, MM) + offsets[b]
    end_out[0, :, :DK] = transit
    end_out[0, :, DK:] = offset


def output_kernel(
    q_ref, map_ref, start_ref, w_ref, u_ref, a_ref, col_ref, gate_ref, gain_ref,
    mixed_out, state_out, fresh_out, gated_out,
):
    count = q_ref.shape[0]
    start = start_ref[0].astype(f32)
    for b in range(count // CHUNK):
        part = slice(b * CHUNK, (b + 1) * CHUNK)
        state = start if b == 0 else fine_dot(map_ref[0, b, :, :DK], start, MM)
        state = state + map_ref[0, b, :, DK:]
        state_out[0, b] = state
        fresh = u_ref[part, :] - fine_dot(w_ref[part, :], state, MM)
        fresh_out[part, :] = fresh
        cum = col_ref[0, part, 1:2]
        mixed_out[part, :] = mm(jnp.exp(cum) * q_ref[part, :], state) + mm(a_ref[0, b], fresh)
    mixed = mixed_out[...]
    gate = gate_ref[...]
    scale = lax.rsqrt(jnp.mean(mixed * mixed, -1, keepdims=True) + head_epsilon)
    gated = mixed * scale * gain_ref[...] * (gate * sigmoid(gate))
    gated_out[...] = gated.astype(bf16)


def tail_back_kernel(
    dgated_ref, mixed_ref, gate_ref, gain_ref, q_ref, a_ref, w_ref, m_ref, col_ref,
    dgate_out, dmixed_out, into_out, own_out, dgain_out,
):
    count = q_ref.shape[0]
    dgated = dgated_ref[...]
    mixed = mixed_ref[...]
    gate = gate_ref[...]
    gain = gain_ref[...]
    sig = sigmoid(gate)
    scale = lax.rsqrt(jnp.mean(mixed * mixed, -1, keepdims=True) + head_epsilon)
    unit = mixed * scale
    dgate = dgated * unit * gain * (sig * (1.0 + gate * (1.0 - sig)))
    dgate_out[...] = dgate.astype(bf16)
    dy = dgated * (gate * sig)
    dgain_out[0] = jnp.sum(dy * unit, 0, keepdims=True)
    dy = dy * gain
    dmixed_out[...] = scale * (dy - unit * jnp.mean(dy * unit, -1, keepdims=True))
    blocks = count // CHUNK
    for b in range(blocks):
        part = slice(b * CHUNK, (b + 1) * CHUNK)
        cum = col_ref[0, part, 1:2]
        reach = jnp.exp(cum) * q_ref[part, :] - mm(a_ref[0, b], w_ref[part, :])
        into_out[0, b] = t_mm(reach, dmixed_out[part, :])
    carried = into_out[0, blocks - 1]
    for b in reversed(range(blocks - 1)):
        carried = fine_dot(m_ref[0, b], carried, T_MM) + into_out[0, b]
    own_out[0] = carried


def conv_back(dact, ext_ref, taps_ref, pad_ref, dext_out, dtaps_out, count):
    width = dact.shape[1]
    conv = convolve(ext_ref, taps_ref, count)
    sig = sigmoid(conv)
    dconv = dact * (sig * (1.0 + conv * (1.0 - sig)))
    pad_ref[0:PAD, :width] = jnp.zeros((PAD, width), f32)
    pad_ref[PAD : PAD + count, :width] = dconv
    pad_ref[PAD + count : PAD + count + 8, :width] = jnp.zeros((8, width), f32)
    total = None
    for j in range(KW):
        term = taps_ref[j : j + 1, :] * pad_ref[KW - 1 - j : KW - 1 - j + PAD + count, :width]
        total = term if total is None else total + term
        start = PAD - KW + 1 + j
        dtaps_out[j : j + 1, :] = jnp.sum(dconv * ext_ref[start : start + count, :], 0, keepdims=True)
    dext_out[...] = total.astype(bf16)


def back_kernel(
    xq, xk, xv, cq, ck, cv, col_ref, row_ref, end_ref, m_ref, into_ref, inv_ref, w_ref, u_ref, a_ref,
    state_ref, fresh_ref, dmixed_ref, q_ref, k_ref,
    dxq, dxk, dxv, dcq, dck, dcv, dcol_out, drow_out,
    dq_ref, dk_ref, dv_ref, pad_ref,
):
    count = q_ref.shape[0]
    rows, cols = places()
    act = convolve(xv, cv, count)
    dv_ref[...] = act * sigmoid(act)
    blocks = count // CHUNK
    ends = [end_ref[0].astype(f32)]
    for b in reversed(range(1, blocks)):
        ends.append(fine_dot(m_ref[0, b], ends[-1], T_MM) + into_ref[0, b])
    ends.reverse()
    is_last = lax.broadcasted_iota(jnp.int32, (CHUNK, 1), 0) == CHUNK - 1
    for b in range(blocks):
        part = slice(b * CHUNK, (b + 1) * CHUNK)
        carried = ends[b]
        beta, cum, decay, last = chunk_decay(col_ref, row_ref, part, rows, cols)
        strict = jnp.where(rows > cols, decay, 0.0)
        key = k_ref[part, :]
        query = q_ref[part, :]
        value = dv_ref[part, :]
        dmixed = dmixed_ref[part, :]
        fresh = fresh_ref[part, :]
        state = state_ref[0, b]
        scores = a_ref[0, b]
        grown = jnp.exp(cum)
        fade = jnp.exp(last - cum)
        tilde = fade * key
        dfresh = t_mm(scores, dmixed) + mm(tilde, carried)
        dscores = mm_t(dmixed, fresh)
        dreach = mm_t(dmixed, state)
        dquery = grown * dreach
        dcum = jnp.sum(dquery * query, -1, keepdims=True)
        gap = dscores * scores
        dinner = dscores * decay
        dq_ref[part, :] = dquery + mm(dinner, key)
        dkey = t_mm(dinner, query)
        dtilde = mm_t(fresh, carried)
        faded = jnp.sum(dtilde * tilde, -1, keepdims=True)
        dkey = dkey + fade * dtilde
        dcum = dcum - faded
        dlast = jnp.sum(faded, 0, keepdims=True) + jnp.exp(last) * jnp.sum(
            jnp.sum(state * carried, -1, keepdims=True), 0, keepdims=True
        )
        dwkey = -mm_t(dfresh, state)
        inverse = inv_ref[0, b]
        dbkey = t_mm(inverse, dwkey)
        dbval = t_mm(inverse, dfresh)
        along = jnp.sum(dbkey * key, -1, keepdims=True) * grown
        dbeta = along + jnp.sum(dbval * value, -1, keepdims=True)
        dcum = dcum + along * beta
        dkey = dkey + (beta * grown) * dbkey
        dv_ref[part, :] = beta * dbval
        dlow = -(mm_t(dbkey, w_ref[part, :]) + mm_t(dbval, u_ref[part, :])) * strict
        inner = mm_t(key, key)
        dbeta = dbeta + jnp.sum(dlow * inner, -1, keepdims=True)
        dlow = dlow * beta
        gap = gap + dlow * inner
        dkey = dkey + mm(dlow, key) + t_mm(dlow, key)
        dk_ref[part, :] = dkey
        dcum = dcum + jnp.sum(gap, -1, keepdims=True) + jnp.where(is_last, dlast, 0.0)
        dcol_out[0, part, 0:1] = dbeta
        dcol_out[0, part, 1:2] = dcum
        drow_out[0, :, part] = -jnp.sum(gap, 0, keepdims=True)
    for ext, taps, d_ref, dext, dtaps, factor in (
        (xq, cq, dq_ref, dxq, dcq, DK ** (-0.5)),
        (xk, ck, dk_ref, dxk, dck, 1.0),
    ):
        act = convolve(ext, taps, count)
        act = act * sigmoid(act)
        scale = lax.rsqrt(jnp.sum(act * act, -1, keepdims=True) + norm_epsilon)
        unit = act * scale
        dunit = d_ref[...] * factor
        dact = scale * (dunit - unit * jnp.sum(unit * dunit, -1, keepdims=True))
        conv_back(dact, ext, taps, pad_ref, dext, dtaps, count)
    conv_back(dv_ref[...], xv, cv, pad_ref, dxv, dcv, count)


class HeadCalls:
    def __init__(self, count, heads):
        self.count, self.heads, self.blocks = count, heads, count // CHUNK
        self.params = pltpu.CompilerParams(
            vmem_limit_bytes=VMEM_LIMIT, dimension_semantics=("arbitrary",)
        )
        h = heads
        ext = count + PAD
        self.ext_specs = [
            pl.BlockSpec((ext, DK), lambda i: (0, i)),
            pl.BlockSpec((ext, DK), lambda i: (0, i + h)),
            pl.BlockSpec((ext, DV), lambda i: (0, i + h)),
        ]
        self.tap_specs = [
            pl.BlockSpec((KW, DK), lambda i: (0, i)),
            pl.BlockSpec((KW, DK), lambda i: (0, i + h)),
            pl.BlockSpec((KW, DV), lambda i: (0, i + h)),
        ]
        self.col = pl.BlockSpec((1, count, 2), lambda i: (i, 0, 0))
        self.row = pl.BlockSpec((1, 1, count), lambda i: (i, 0, 0))
        self.gain = pl.BlockSpec((1, DV), lambda i: (0, 0))

    def wide(self, width):
        return pl.BlockSpec((self.count, width), lambda i: (0, i))

    def stack(self, *shape):
        return pl.BlockSpec((1,) + shape, lambda i: (i,) + (0,) * len(shape))

    def wide_shape(self, width, dtype=f32):
        return jax.ShapeDtypeStruct((self.count, self.heads * width), dtype)

    def stack_shape(self, *shape, dtype=f32):
        return jax.ShapeDtypeStruct((self.heads,) + shape, dtype)

    def call(self, kernel, in_specs, out_specs, out_shape, name, scratch=()):
        return pl.pallas_call(
            kernel,
            grid=(self.heads,),
            in_specs=in_specs,
            out_specs=out_specs,
            out_shape=out_shape,
            scratch_shapes=list(scratch),
            compiler_params=self.params,
            name=name,
        )

    def front(self, ext, taps, col, row):
        nb = self.blocks
        return self.call(
            front_kernel,
            self.ext_specs + self.tap_specs + [self.col, self.row],
            [
                self.wide(DK), self.wide(DK), self.stack(nb, CHUNK, CHUNK), self.wide(DK), self.wide(DV),
                self.stack(nb, CHUNK, CHUNK), self.stack(nb, DK, DK), self.stack(nb, DK, DK + DV),
                self.stack(DK, DK + DV),
            ],
            [
                self.wide_shape(DK), self.wide_shape(DK), self.stack_shape(nb, CHUNK, CHUNK),
                self.wide_shape(DK), self.wide_shape(DV), self.stack_shape(nb, CHUNK, CHUNK),
                self.stack_shape(nb, DK, DK), self.stack_shape(nb, DK, DK + DV),
                self.stack_shape(DK, DK + DV),
            ],
            "delta_front",
        )(ext, ext, ext, taps, taps, taps, col, row)

    def outputs(self, query, maps, start, wkey, wval, scores, col, gate_pre, gain):
        nb = self.blocks
        return self.call(
            output_kernel,
            [
                self.wide(DK), self.stack(nb, DK, DK + DV), self.stack(DK, DV), self.wide(DK), self.wide(DV),
                self.stack(nb, CHUNK, CHUNK), self.col, self.wide(DV), self.gain,
            ],
            [self.wide(DV), self.stack(nb, DK, DV), self.wide(DV), self.wide(DV)],
            [
                self.wide_shape(DV), self.stack_shape(nb, DK, DV), self.wide_shape(DV),
                self.wide_shape(DV, bf16),
            ],
            "delta_outputs",
        )(query, maps, start, wkey, wval, scores, col, gate_pre, gain)

    def tail_back(self, dgated, mixed, gate_pre, gain, query, scores, wkey, steps, col):
        nb = self.blocks
        return self.call(
            tail_back_kernel,
            [
                self.wide(DV), self.wide(DV), self.wide(DV), self.gain, self.wide(DK),
                self.stack(nb, CHUNK, CHUNK), self.wide(DK), self.stack(nb, DK, DK), self.col,
            ],
            [
                self.wide(DV), self.wide(DV), self.stack(nb, DK, DV), self.stack(DK, DV),
                self.stack(1, DV),
            ],
            [
                self.wide_shape(DV, bf16), self.wide_shape(DV), self.stack_shape(nb, DK, DV),
                self.stack_shape(DK, DV), self.stack_shape(1, DV),
            ],
            "delta_tail_back",
        )(dgated, mixed, gate_pre, gain, query, scores, wkey, steps, col)

    def back(self, ext, taps, col, row, end, steps, into, inverse, wkey, wval, scores, states, fresh, dmixed, query, key):
        nb, count, heads = self.blocks, self.count, self.heads
        rows = count + PAD
        square = self.stack(nb, CHUNK, CHUNK)
        return self.call(
            back_kernel,
            self.ext_specs + self.tap_specs + [
                self.col, self.row, self.stack(DK, DV), self.stack(nb, DK, DK), self.stack(nb, DK, DV),
                square, self.wide(DK), self.wide(DV), square, self.stack(nb, DK, DV), self.wide(DV),
                self.wide(DV), self.wide(DK), self.wide(DK),
            ],
            [
                pl.BlockSpec((rows, DK), lambda i: (0, i)), pl.BlockSpec((rows, DK), lambda i: (0, i)),
                pl.BlockSpec((rows, DV), lambda i: (0, i)), pl.BlockSpec((KW, DK), lambda i: (0, i)),
                pl.BlockSpec((KW, DK), lambda i: (0, i)), pl.BlockSpec((KW, DV), lambda i: (0, i)),
                self.col, self.row,
            ],
            [
                jax.ShapeDtypeStruct((rows, heads * DK), bf16), jax.ShapeDtypeStruct((rows, heads * DK), bf16),
                jax.ShapeDtypeStruct((rows, heads * DV), bf16), jax.ShapeDtypeStruct((KW, heads * DK), f32),
                jax.ShapeDtypeStruct((KW, heads * DK), f32), jax.ShapeDtypeStruct((KW, heads * DV), f32),
                jax.ShapeDtypeStruct((heads, count, 2), f32), jax.ShapeDtypeStruct((heads, 1, count), f32),
            ],
            "delta_back",
            [
                pltpu.VMEM((count, DK), f32), pltpu.VMEM((count, DK), f32), pltpu.VMEM((count, DV), f32),
                pltpu.VMEM((PAD + count + 8, DV), f32),
            ],
        )(
            ext, ext, ext, taps, taps, taps, col, row, end, steps, into, inverse, wkey, wval, scores,
            states, fresh, dmixed, query, key,
        )


def rep_piece(block, rows):
    return lax.dynamic_slice_in_dim(block, lax.axis_index("rep") * rows, rows, 0)


def gather_everywhere(block):
    return lax.all_gather(block, ("fsdp", "rep"), axis=0, tiled=True)


def passed_along(block, distance):
    devices = range(lax.axis_size("fsdp"))
    route = [(i - distance, i) for i in devices if i - distance in devices]
    return lax.ppermute(block, "fsdp", route)


def carried_states(transit, offset, backward):
    count = lax.axis_size("fsdp")
    carried = jnp.zeros_like(offset)
    for hop in range(count - 1):
        source = count - 1 - hop if backward else hop
        target = source - 1 if backward else source + 1
        moved = offset
        if hop:
            form = "hed,hef->hdf" if backward else "hde,hef->hdf"
            moved = moved + jnp.einsum(form, transit, carried, preferred_element_type=f32)
        arrived = lax.ppermute(moved.astype(bf16), "fsdp", [(source, target)])
        carried = carried + arrived.astype(f32)
    return carried


def partners(bit):
    return [(i, i ^ bit) for i in range(lax.axis_size("rep"))]


def halves(block, axis, bit):
    mine = (lax.axis_index("rep") // bit) % 2
    return (
        lax.dynamic_index_in_dim(block, mine, axis, keepdims=False),
        lax.dynamic_index_in_dim(block, 1 - mine, axis, keepdims=False),
    )


def halve(block, axis, bit):
    kept, sent = halves(block, axis, bit)
    return kept + lax.ppermute(sent, "rep", partners(bit))


def sum_to_owners(grads):
    owners, reps = lax.axis_size("fsdp"), lax.axis_size("rep")
    levels = reps.bit_length() - 1
    width = grads[0].shape[1]
    sizes = [grad.shape[0] // (owners * reps) for grad in grads]
    pairs = [
        halves(grad.reshape((owners,) + (2,) * levels + (size, width)), levels, 1)
        for grad, size in zip(grads, sizes)
    ]
    kept, sent = [jnp.concatenate(side, -2) for side in zip(*pairs)]
    block = kept + lax.ppermute(sent, "rep", partners(1))
    left = block[..., : width // 2]
    right = block[..., width // 2 :]
    for level in range(1, levels):
        left = halve(left, levels - level, 1 << level)
        right = halve(right, 1, 1 << (levels - level))
    block = jnp.concatenate([left, right], -1).reshape(-1, width)
    block = lax.psum_scatter(block, "fsdp", scatter_dimension=0, tiled=True)
    block = lax.all_gather(block, "rep", axis=0)
    sums, at = [], 0
    for size in sizes:
        sums.append(block[:, at : at + size].reshape(-1, width).astype(f32))
        at += size
    return sums


def sum_everywhere(block):
    for axis in ("rep", "fsdp"):
        size = lax.axis_size(axis)
        bit = 1
        while bit < size:
            block = block + lax.ppermute(block, axis, [(i, i ^ bit) for i in range(size)])
            bit *= 2
    return block


def matmul_low(left, right):
    return jnp.dot(left, right, preferred_element_type=f32)


def matmul_high(left, right):
    return jnp.dot(left, right, precision=highest, preferred_element_type=f32)


def matmul_nt(left, right):
    return lax.dot_general(left, right, (((1,), (1,)), ((), ())), preferred_element_type=f32)


def matmul_tn(left, right):
    return lax.dot_general(left, right, (((0,), (0,)), ((), ())), preferred_element_type=f32)


def rms_scale(values, gain):
    return values * lax.rsqrt(jnp.mean(values * values, -1, keepdims=True) + norm_epsilon) * gain


def swiglu(ff_gate, ff_up):
    return jax.nn.silu(ff_gate) * ff_up


def head_gates(beta_pre, decay_pre, a_log, dt_bias, valid_mask):
    row_count, head_count = beta_pre.shape
    beta_gate = valid_mask * jax.nn.sigmoid(beta_pre)
    log_decay = -valid_mask * jnp.exp(a_log) * jax.nn.softplus(decay_pre + dt_bias)
    cum_log = jnp.cumsum(log_decay.reshape(row_count // CHUNK, CHUNK, head_count), 1)
    return beta_gate, cum_log.reshape(row_count, head_count)


def on_device(
    tokens, cotangent, valid_count, norm_mix, w_query, w_key, w_value, w_gate, w_beta, w_decay,
    a_log, dt_bias, conv_weight, norm_head, w_out, norm_ffn, w_ffgate, w_ffup, w_ffdown,
):
    row_count, width = tokens.shape
    head_count = a_log.shape[0]
    owners, reps = lax.axis_size("fsdp"), lax.axis_size("rep")
    qk_width = head_count * DK
    own_count = valid_count[0, 0]
    valid_mask = (jnp.arange(row_count) < own_count).astype(f32)[:, None]

    share = w_query.shape[0] // reps
    w_qkv = gather_everywhere(
        jnp.concatenate([rep_piece(w, share) for w in (w_query, w_key, w_value)], 1)
    )
    gate_pieces = rep_piece(w_gate, share)
    parts = [
        gate_pieces[:, :width],
        gate_pieces[:, width:],
        rep_piece(w_out, w_out.shape[0] // reps),
        rep_piece(w_ffgate.T, w_ffgate.shape[1] // reps),
        rep_piece(w_ffup.T, w_ffup.shape[1] // reps),
        rep_piece(w_ffdown, w_ffdown.shape[0] // reps),
    ]
    packed, w_qkv = lax.optimization_barrier((jnp.concatenate(parts, 0), w_qkv))
    rest = gather_everywhere(packed).reshape(owners * reps, -1, width)
    whole, at = [], 0
    for part in parts:
        whole.append(rest[:, at : at + part.shape[0]].reshape(-1, width))
        at += part.shape[0]
    gate_left, gate_right, out_full, ffgate_t, ffup_t, ffdown_full = whole

    small = [norm_mix, norm_ffn, norm_head, w_beta.reshape(-1), w_decay.reshape(-1), conv_weight.reshape(-1)]
    small_full = lax.all_gather(jnp.concatenate(small), "fsdp", axis=0)
    at, pieces = 0, []
    for part in small:
        pieces.append(small_full[:, at : at + part.shape[0]])
        at += part.shape[0]
    mix_gain, ffn_gain, head_gain = [p.reshape(-1).astype(f32) for p in pieces[:3]]
    w_beta_decay = jnp.concatenate([p.reshape(width, head_count) for p in pieces[3:5]], 1)
    taps = pieces[5].reshape(owners, KW, -1).transpose(1, 0, 2).reshape(KW, -1).astype(f32)
    head_gain = head_gain[None, :]

    inputs = tokens.astype(f32)
    edge_place = own_count - (KW - 1)
    before = passed_along(lax.dynamic_slice_in_dim(tokens, edge_place, KW - 1, 0), 1)
    ahead = jnp.concatenate([jnp.zeros((PAD - KW + 1, width), f32), before.astype(f32)], 0)
    normed_f32, mix_pull = jax.vjp(rms_scale, inputs, mix_gain)
    normed = normed_f32.astype(bf16)
    normed_ext = jnp.concatenate([rms_scale(ahead, mix_gain).astype(bf16), normed], 0)
    projected = matmul_low(normed_ext, w_qkv)
    gates_pre = matmul_low(normed, w_beta_decay)
    beta_pre, decay_pre = gates_pre[:, :head_count], gates_pre[:, head_count:]
    (beta_gate, cum_log), gates_pull = jax.vjp(
        lambda *args: head_gates(*args, valid_mask), beta_pre, decay_pre, a_log, dt_bias
    )
    col = jnp.stack([beta_gate.T, cum_log.T], -1)
    row = cum_log.T[:, None, :]
    calls = HeadCalls(row_count, head_count)
    query, key, inverse, wkey, wval, scores, steps, maps, end_map = calls.front(projected, taps, col, row)
    transit = end_map[:, :, :DK]
    start_state = carried_states(transit, end_map[:, :, DK:], False)
    gate_pre = jnp.concatenate([matmul_low(normed, gate_left), matmul_low(normed, gate_right)], 1)
    mixed, states, fresh, gated_out = calls.outputs(
        query, maps, start_state, wkey, wval, scores, col, gate_pre, head_gain
    )
    residual = inputs + matmul_low(gated_out, out_full)

    ffn_f32, ffn_pull = jax.vjp(rms_scale, residual, ffn_gain)
    normed_ffn = ffn_f32.astype(bf16)
    swiglu_f32, swiglu_pull = jax.vjp(
        swiglu, matmul_nt(normed_ffn, ffgate_t), matmul_nt(normed_ffn, ffup_t)
    )
    swiglu_out = swiglu_f32.astype(bf16)
    output = (valid_mask * (residual + matmul_low(swiglu_out, ffdown_full))).astype(bf16)
    out_grad = cotangent.astype(f32) * valid_mask
    out_low = out_grad.astype(bf16)
    gate_grad_f32, up_grad_f32 = swiglu_pull(matmul_nt(out_low, ffdown_full))
    gate_low = gate_grad_f32.astype(bf16)
    up_low = up_grad_f32.astype(bf16)
    ffn_in_grad = matmul_low(gate_low, ffgate_t) + matmul_low(up_low, ffup_t)
    residual_part, ffn_gain_grad = ffn_pull(ffn_in_grad)
    residual_grad = out_grad + residual_part
    residual_low = residual_grad.astype(bf16)

    dgated = matmul_nt(residual_low, out_full)
    dgate_low, dmixed, into, own_grad, dgain = calls.tail_back(
        dgated, mixed, gate_pre, head_gain, query, scores, wkey, steps, col
    )
    end_grad = carried_states(transit, own_grad, True)

    ffdown_grad, ffgate_grad, ffup_grad = sum_to_owners([
        matmul_tn(swiglu_out, out_low).astype(bf16),
        matmul_tn(gate_low, normed_ffn).astype(bf16),
        matmul_tn(up_low, normed_ffn).astype(bf16),
    ])
    out_weight_grad, gate_left_grad, gate_right_grad = sum_to_owners([
        matmul_tn(gated_out, residual_low).astype(bf16),
        matmul_tn(normed, dgate_low[:, :width]).astype(bf16),
        matmul_tn(normed, dgate_low[:, width:]).astype(bf16),
    ])

    dxq, dxk, dxv, dtap_q, dtap_k, dtap_v, dcol, drow = calls.back(
        projected, taps, col, row, end_grad, steps, into, inverse, wkey, wval, scores, states, fresh,
        dmixed, query, key,
    )
    dprojected = jnp.concatenate([dxq, dxk, dxv], 1)
    (qkv_grad,) = sum_to_owners([matmul_tn(normed_ext, dprojected).astype(bf16)])
    coming = passed_along(dprojected[PAD - KW + 1 : PAD], -1)
    own_low = dprojected[PAD:]
    edge_rows = lax.dynamic_slice_in_dim(own_low, edge_place, KW - 1, 0).astype(f32) + coming.astype(f32)
    own_low = lax.dynamic_update_slice_in_dim(own_low, edge_rows.astype(bf16), edge_place, 0)
    beta_pre_grad, decay_pre_grad, rate_grad, bias_grad = gates_pull(
        (dcol[:, :, 0].T, (dcol[:, :, 1] + drow[:, 0, :]).T)
    )
    gates_grad = jnp.concatenate([beta_pre_grad, decay_pre_grad], 1)
    normed_grad = (
        matmul_nt(own_low, w_qkv)
        + matmul_nt(dgate_low[:, :width], gate_left)
        + matmul_nt(dgate_low[:, width:], gate_right)
        + matmul_high(gates_grad, w_beta_decay.astype(f32).T)
    )
    input_part, mix_gain_grad = mix_pull(normed_grad)
    grad_tokens = residual_grad + input_part

    gates_weight_grad = lax.dot_general(
        normed.astype(f32), gates_grad, (((0,), (0,)), ((), ())), precision=highest,
        preferred_element_type=f32,
    )
    dtaps = jnp.concatenate([dtap_q, dtap_k, dtap_v], 1)
    small = [
        mix_gain_grad, ffn_gain_grad, jnp.sum(dgain, 0).reshape(-1), gates_weight_grad.reshape(-1),
        dtaps.reshape(-1), rate_grad, bias_grad,
    ]
    flat = jnp.concatenate(small)
    lanes = 128
    flat = jnp.pad(flat, (0, -flat.shape[0] % (8 * lanes))).reshape(-1, lanes)
    sums = sum_everywhere(flat).reshape(-1)
    at, pieces = 0, []
    for part in small:
        pieces.append(sums[at : at + part.shape[0]])
        at += part.shape[0]
    mine = lax.axis_index("fsdp")

    def own(block, axis):
        size = block.shape[axis] // owners
        return lax.dynamic_slice_in_dim(block, mine * size, size, axis)

    gates_weight = own(pieces[3].reshape(width, 2 * head_count), 0)
    return (
        output,
        grad_tokens,
        own(pieces[0], 0),
        qkv_grad[:, :qk_width],
        qkv_grad[:, qk_width : 2 * qk_width],
        qkv_grad[:, 2 * qk_width :],
        jnp.concatenate([gate_left_grad, gate_right_grad], 1),
        gates_weight[:, :head_count],
        gates_weight[:, head_count:],
        pieces[5],
        pieces[6],
        own(pieces[4].reshape(KW, -1), 1),
        own(pieces[2], 0),
        out_weight_grad,
        own(pieces[1], 0),
        ffgate_grad.T,
        ffup_grad.T,
        ffdown_grad,
    )


def solution(mesh):
    rows = P(("rep", "fsdp"), None)
    first, second, vector = P("fsdp", None), P(None, "fsdp"), P("fsdp")
    placed = (
        rows, rows, P("rep", "fsdp"), vector, first, first, first, first, first, first, P(), P(),
        second, vector, first, vector, second, second, first,
    )
    given = (
        rows, rows, vector, first, first, first, first, first, first, P(), P(), second, vector, first,
        vector, second, second, first,
    )
    return jax.shard_map(on_device, mesh=mesh, in_specs=placed, out_specs=given, check_vma=False)
```

```python
import functools

import jax
import jax.numpy as jnp
from jax import lax
from jax.experimental import pallas as pl
from jax.experimental.pallas import tpu as pltpu
from jax.sharding import PartitionSpec as P

DK = 128
DV = 256
KW = 4
CHUNK = 128
PAD = 16
VMEM_LIMIT = 56 * 1024 * 1024

norm_epsilon = 1e-06
head_epsilon = 1e-05
highest = lax.Precision.HIGHEST
f32 = jnp.float32
bf16 = jnp.bfloat16


MM, MM_T, T_MM = ((1,), (0,)), ((1,), (1,)), ((0,), (0,))


def low_dot(a, b, dims):
    return lax.dot_general(a.astype(bf16), b.astype(bf16), (dims, ((), ())), preferred_element_type=f32)


def fine_dot(a, b, dims):
    a_high, b_high = a.astype(bf16), b.astype(bf16)
    a_low = (a - a_high.astype(f32)).astype(bf16)
    b_low = (b - b_high.astype(f32)).astype(bf16)
    return (
        low_dot(a_high, b_high, dims) + low_dot(a_high, b_low, dims) + low_dot(a_low, b_high, dims)
    )


def mm(a, b):
    return low_dot(a, b, MM)


def mm_t(a, b):
    return low_dot(a, b, MM_T)


def t_mm(a, b):
    return low_dot(a, b, T_MM)


def places():
    rows = lax.broadcasted_iota(jnp.int32, (CHUNK, CHUNK), 0)
    cols = lax.broadcasted_iota(jnp.int32, (CHUNK, CHUNK), 1)
    return rows, cols


def unit_lower_inverses(lows, rows, cols):
    differ = rows ^ cols
    eye = jnp.where(rows == cols, 1.0, 0.0)
    inverses = [eye - jnp.where(differ == 1, low, 0.0) for low in lows]
    size = 2
    while size < CHUNK:
        off = (differ >= size) & (differ < 2 * size)
        inner = [fine_dot(jnp.where(off, low, 0.0), inv, MM) for low, inv in zip(lows, inverses)]
        inverses = [inv - fine_dot(inv, part, MM) for inv, part in zip(inverses, inner)]
        size *= 2
    return inverses


def convolve(ext_ref, taps_ref, count):
    total = taps_ref[0:1, :] * ext_ref[PAD - KW + 1 : PAD - KW + 1 + count, :]
    for j in range(1, KW):
        start = PAD - KW + 1 + j
        total = total + taps_ref[j : j + 1, :] * ext_ref[start : start + count, :]
    return total


def sigmoid(z):
    return 1.0 / (1.0 + jnp.exp(-z))


def chunk_decay(col_ref, row_ref, part, rows, cols):
    beta = col_ref[0, part, 0:1]
    cum = col_ref[0, part, 1:2]
    gap = cum - row_ref[0, :, part]
    decay = jnp.where(rows >= cols, jnp.exp(jnp.minimum(gap, 0.0)), 0.0)
    last = cum[CHUNK - 1 : CHUNK, :]
    return beta, cum, decay, last


def front_kernel(
    xq, xk, xv, cq, ck, cv, col_ref, row_ref,
    q_out, k_out, inv_out, w_out, u_out, a_out, m_out, map_out, end_out,
):
    count = q_out.shape[0]
    rows, cols = places()
    eye = jnp.where(rows == cols, 1.0, 0.0)
    act = convolve(xq, cq, count)
    act = act * sigmoid(act)
    q_out[...] = act * lax.rsqrt(jnp.sum(act * act, -1, keepdims=True) + norm_epsilon) * DK ** (-0.5)
    act = convolve(xk, ck, count)
    act = act * sigmoid(act)
    k_out[...] = act * lax.rsqrt(jnp.sum(act * act, -1, keepdims=True) + norm_epsilon)
    act = convolve(xv, cv, count)
    values = act * sigmoid(act)
    blocks = range(count // CHUNK)
    parts = [slice(b * CHUNK, (b + 1) * CHUNK) for b in blocks]
    gates = [chunk_decay(col_ref, row_ref, part, rows, cols) for part in parts]
    keys = [k_out[part, :] for part in parts]
    lows = [
        beta * fine_dot(key, key, MM_T) * jnp.where(rows > cols, decay, 0.0)
        for key, (beta, _, decay, _) in zip(keys, gates)
    ]
    inverses = unit_lower_inverses(lows, rows, cols)
    steps, offsets = [], []
    for b, part, key, inverse, (beta, cum, decay, last) in zip(blocks, parts, keys, inverses, gates):
        inv_out[0, b] = inverse
        wkey = fine_dot(inverse, beta * jnp.exp(cum) * key, MM)
        wval = fine_dot(inverse, beta * values[part, :], MM)
        w_out[part, :] = wkey
        u_out[part, :] = wval
        a_out[0, b] = mm_t(q_out[part, :], key) * decay
        tilde = jnp.exp(last - cum) * key
        step = jnp.exp(last) * eye - t_mm(tilde, wkey)
        m_out[0, b] = step
        steps.append(step)
        offsets.append(t_mm(tilde, wval))
    transit, offset = eye, jnp.zeros((DK, DV), f32)
    for b in blocks:
        map_out[0, b, :, :DK] = transit
        map_out[0, b, :, DK:] = offset
        if b == 0:
            transit, offset = steps[0], offsets[0]
        else:
            transit, offset = fine_dot(steps[b], transit, MM), fine_dot(steps[b], offset, MM) + offsets[b]
    end_out[0, :, :DK] = transit
    end_out[0, :, DK:] = offset


def output_kernel(
    q_ref, map_ref, start_ref, w_ref, u_ref, a_ref, col_ref, gate_ref, gain_ref,
    mixed_out, state_out, fresh_out, gated_out,
):
    count = q_ref.shape[0]
    start = start_ref[0].astype(f32)
    for b in range(count // CHUNK):
        part = slice(b * CHUNK, (b + 1) * CHUNK)
        state = start if b == 0 else fine_dot(map_ref[0, b, :, :DK], start, MM)
        state = state + map_ref[0, b, :, DK:]
        state_out[0, b] = state
        fresh = u_ref[part, :] - fine_dot(w_ref[part, :], state, MM)
        fresh_out[part, :] = fresh
        cum = col_ref[0, part, 1:2]
        mixed_out[part, :] = mm(jnp.exp(cum) * q_ref[part, :], state) + mm(a_ref[0, b], fresh)
    mixed = mixed_out[...]
    gate = gate_ref[...]
    scale = lax.rsqrt(jnp.mean(mixed * mixed, -1, keepdims=True) + head_epsilon)
    gated = mixed * scale * gain_ref[...] * (gate * sigmoid(gate))
    gated_out[...] = gated.astype(bf16)


def tail_back_kernel(
    dgated_ref, mixed_ref, gate_ref, gain_ref, q_ref, a_ref, w_ref, m_ref, col_ref,
    dgate_out, dmixed_out, into_out, own_out, dgain_out,
):
    count = q_ref.shape[0]
    dgated = dgated_ref[...]
    mixed = mixed_ref[...]
    gate = gate_ref[...]
    gain = gain_ref[...]
    sig = sigmoid(gate)
    scale = lax.rsqrt(jnp.mean(mixed * mixed, -1, keepdims=True) + head_epsilon)
    unit = mixed * scale
    dgate = dgated * unit * gain * (sig * (1.0 + gate * (1.0 - sig)))
    dgate_out[...] = dgate.astype(bf16)
    dy = dgated * (gate * sig)
    dgain_out[0] = jnp.sum(dy * unit, 0, keepdims=True)
    dy = dy * gain
    dmixed_out[...] = scale * (dy - unit * jnp.mean(dy * unit, -1, keepdims=True))
    blocks = count // CHUNK
    for b in range(blocks):
        part = slice(b * CHUNK, (b + 1) * CHUNK)
        cum = col_ref[0, part, 1:2]
        reach = jnp.exp(cum) * q_ref[part, :] - mm(a_ref[0, b], w_ref[part, :])
        into_out[0, b] = t_mm(reach, dmixed_out[part, :])
    carried = into_out[0, blocks - 1]
    for b in reversed(range(blocks - 1)):
        carried = fine_dot(m_ref[0, b], carried, T_MM) + into_out[0, b]
    own_out[0] = carried


def conv_back(dact, ext_ref, taps_ref, pad_ref, dext_out, dtaps_out, count):
    width = dact.shape[1]
    conv = convolve(ext_ref, taps_ref, count)
    sig = sigmoid(conv)
    dconv = dact * (sig * (1.0 + conv * (1.0 - sig)))
    pad_ref[0:PAD, :width] = jnp.zeros((PAD, width), f32)
    pad_ref[PAD : PAD + count, :width] = dconv
    pad_ref[PAD + count : PAD + count + 8, :width] = jnp.zeros((8, width), f32)
    total = None
    for j in range(KW):
        term = taps_ref[j : j + 1, :] * pad_ref[KW - 1 - j : KW - 1 - j + PAD + count, :width]
        total = term if total is None else total + term
        start = PAD - KW + 1 + j
        dtaps_out[j : j + 1, :] = jnp.sum(dconv * ext_ref[start : start + count, :], 0, keepdims=True)
    dext_out[...] = total.astype(bf16)


def back_kernel(
    xq, xk, xv, cq, ck, cv, col_ref, row_ref, end_ref, m_ref, into_ref, inv_ref, w_ref, u_ref, a_ref,
    state_ref, fresh_ref, dmixed_ref, q_ref, k_ref,
    dxq, dxk, dxv, dcq, dck, dcv, dcol_out, drow_out,
    dq_ref, dk_ref, dv_ref, pad_ref,
):
    count = q_ref.shape[0]
    rows, cols = places()
    act = convolve(xv, cv, count)
    dv_ref[...] = act * sigmoid(act)
    blocks = count // CHUNK
    ends = [end_ref[0].astype(f32)]
    for b in reversed(range(1, blocks)):
        ends.append(fine_dot(m_ref[0, b], ends[-1], T_MM) + into_ref[0, b])
    ends.reverse()
    is_last = lax.broadcasted_iota(jnp.int32, (CHUNK, 1), 0) == CHUNK - 1
    for b in range(blocks):
        part = slice(b * CHUNK, (b + 1) * CHUNK)
        carried = ends[b]
        beta, cum, decay, last = chunk_decay(col_ref, row_ref, part, rows, cols)
        strict = jnp.where(rows > cols, decay, 0.0)
        key = k_ref[part, :]
        query = q_ref[part, :]
        value = dv_ref[part, :]
        dmixed = dmixed_ref[part, :]
        fresh = fresh_ref[part, :]
        state = state_ref[0, b]
        scores = a_ref[0, b]
        grown = jnp.exp(cum)
        fade = jnp.exp(last - cum)
        tilde = fade * key
        dfresh = t_mm(scores, dmixed) + mm(tilde, carried)
        dscores = mm_t(dmixed, fresh)
        dreach = mm_t(dmixed, state)
        dquery = grown * dreach
        dcum = jnp.sum(dquery * query, -1, keepdims=True)
        gap = dscores * scores
        dinner = dscores * decay
        dq_ref[part, :] = dquery + mm(dinner, key)
        dkey = t_mm(dinner, query)
        dtilde = mm_t(fresh, carried)
        faded = jnp.sum(dtilde * tilde, -1, keepdims=True)
        dkey = dkey + fade * dtilde
        dcum = dcum - faded
        dlast = jnp.sum(faded, 0, keepdims=True) + jnp.exp(last) * jnp.sum(
            jnp.sum(state * carried, -1, keepdims=True), 0, keepdims=True
        )
        dwkey = -mm_t(dfresh, state)
        inverse = inv_ref[0, b]
        dbkey = t_mm(inverse, dwkey)
        dbval = t_mm(inverse, dfresh)
        along = jnp.sum(dbkey * key, -1, keepdims=True) * grown
        dbeta = along + jnp.sum(dbval * value, -1, keepdims=True)
        dcum = dcum + along * beta
        dkey = dkey + (beta * grown) * dbkey
        dv_ref[part, :] = beta * dbval
        dlow = -(mm_t(dbkey, w_ref[part, :]) + mm_t(dbval, u_ref[part, :])) * strict
        inner = mm_t(key, key)
        dbeta = dbeta + jnp.sum(dlow * inner, -1, keepdims=True)
        dlow = dlow * beta
        gap = gap + dlow * inner
        dkey = dkey + mm(dlow, key) + t_mm(dlow, key)
        dk_ref[part, :] = dkey
        dcum = dcum + jnp.sum(gap, -1, keepdims=True) + jnp.where(is_last, dlast, 0.0)
        dcol_out[0, part, 0:1] = dbeta
        dcol_out[0, part, 1:2] = dcum
        drow_out[0, :, part] = -jnp.sum(gap, 0, keepdims=True)
    for ext, taps, d_ref, dext, dtaps, factor in (
        (xq, cq, dq_ref, dxq, dcq, DK ** (-0.5)),
        (xk, ck, dk_ref, dxk, dck, 1.0),
    ):
        act = convolve(ext, taps, count)
        act = act * sigmoid(act)
        scale = lax.rsqrt(jnp.sum(act * act, -1, keepdims=True) + norm_epsilon)
        unit = act * scale
        dunit = d_ref[...] * factor
        dact = scale * (dunit - unit * jnp.sum(unit * dunit, -1, keepdims=True))
        conv_back(dact, ext, taps, pad_ref, dext, dtaps, count)
    conv_back(dv_ref[...], xv, cv, pad_ref, dxv, dcv, count)


class HeadCalls:
    def __init__(self, count, heads):
        self.count, self.heads, self.blocks = count, heads, count // CHUNK
        self.params = pltpu.CompilerParams(
            vmem_limit_bytes=VMEM_LIMIT, dimension_semantics=("arbitrary",)
        )
        h = heads
        ext = count + PAD
        self.ext_specs = [
            pl.BlockSpec((ext, DK), lambda i: (0, i)),
            pl.BlockSpec((ext, DK), lambda i: (0, i + h)),
            pl.BlockSpec((ext, DV), lambda i: (0, i + h)),
        ]
        self.tap_specs = [
            pl.BlockSpec((KW, DK), lambda i: (0, i)),
            pl.BlockSpec((KW, DK), lambda i: (0, i + h)),
            pl.BlockSpec((KW, DV), lambda i: (0, i + h)),
        ]
        self.col = pl.BlockSpec((1, count, 2), lambda i: (i, 0, 0))
        self.row = pl.BlockSpec((1, 1, count), lambda i: (i, 0, 0))
        self.gain = pl.BlockSpec((1, DV), lambda i: (0, 0))

    def wide(self, width):
        return pl.BlockSpec((self.count, width), lambda i: (0, i))

    def stack(self, *shape):
        return pl.BlockSpec((1,) + shape, lambda i: (i,) + (0,) * len(shape))

    def wide_shape(self, width, dtype=f32):
        return jax.ShapeDtypeStruct((self.count, self.heads * width), dtype)

    def stack_shape(self, *shape, dtype=f32):
        return jax.ShapeDtypeStruct((self.heads,) + shape, dtype)

    def call(self, kernel, in_specs, out_specs, out_shape, name, micros, scratch=()):
        return pl.pallas_call(
            kernel,
            grid=(self.heads,),
            in_specs=in_specs,
            out_specs=out_specs,
            out_shape=out_shape,
            scratch_shapes=list(scratch),
            compiler_params=self.params,
            cost_estimate=pl.CostEstimate(
                flops=0, transcendentals=0, bytes_accessed=micros * self.count * self.heads * 768
            ),
            name=name,
        )

    def front(self, ext, taps, col, row):
        nb = self.blocks
        return self.call(
            front_kernel,
            self.ext_specs + self.tap_specs + [self.col, self.row],
            [
                self.wide(DK), self.wide(DK), self.stack(nb, CHUNK, CHUNK), self.wide(DK), self.wide(DV),
                self.stack(nb, CHUNK, CHUNK), self.stack(nb, DK, DK), self.stack(nb, DK, DK + DV),
                self.stack(DK, DK + DV),
            ],
            [
                self.wide_shape(DK), self.wide_shape(DK), self.stack_shape(nb, CHUNK, CHUNK),
                self.wide_shape(DK), self.wide_shape(DV), self.stack_shape(nb, CHUNK, CHUNK),
                self.stack_shape(nb, DK, DK), self.stack_shape(nb, DK, DK + DV),
                self.stack_shape(DK, DK + DV),
            ],
            "delta_front",
            41,
        )(ext, ext, ext, taps, taps, taps, col, row)

    def outputs(self, query, maps, start, wkey, wval, scores, col, gate_pre, gain):
        nb = self.blocks
        return self.call(
            output_kernel,
            [
                self.wide(DK), self.stack(nb, DK, DK + DV), self.stack(DK, DV), self.wide(DK), self.wide(DV),
                self.stack(nb, CHUNK, CHUNK), self.col, self.wide(DV), self.gain,
            ],
            [self.wide(DV), self.stack(nb, DK, DV), self.wide(DV), self.wide(DV)],
            [
                self.wide_shape(DV), self.stack_shape(nb, DK, DV), self.wide_shape(DV),
                self.wide_shape(DV, bf16),
            ],
            "delta_outputs",
            18,
        )(query, maps, start, wkey, wval, scores, col, gate_pre, gain)

    def tail_back(self, dgated, mixed, gate_pre, gain, query, scores, wkey, steps, col):
        nb = self.blocks
        return self.call(
            tail_back_kernel,
            [
                self.wide(DV), self.wide(DV), self.wide(DV), self.gain, self.wide(DK),
                self.stack(nb, CHUNK, CHUNK), self.wide(DK), self.stack(nb, DK, DK), self.col,
            ],
            [
                self.wide(DV), self.wide(DV), self.stack(nb, DK, DV), self.stack(DK, DV),
                self.stack(1, DV),
            ],
            [
                self.wide_shape(DV, bf16), self.wide_shape(DV), self.stack_shape(nb, DK, DV),
                self.stack_shape(DK, DV), self.stack_shape(1, DV),
            ],
            "delta_tail_back",
            17,
        )(dgated, mixed, gate_pre, gain, query, scores, wkey, steps, col)

    def back(self, ext, taps, col, row, end, steps, into, inverse, wkey, wval, scores, states, fresh, dmixed, query, key):
        nb, count, heads = self.blocks, self.count, self.heads
        rows = count + PAD
        square = self.stack(nb, CHUNK, CHUNK)
        return self.call(
            back_kernel,
            self.ext_specs + self.tap_specs + [
                self.col, self.row, self.stack(DK, DV), self.stack(nb, DK, DK), self.stack(nb, DK, DV),
                square, self.wide(DK), self.wide(DV), square, self.stack(nb, DK, DV), self.wide(DV),
                self.wide(DV), self.wide(DK), self.wide(DK),
            ],
            [
                pl.BlockSpec((rows, DK), lambda i: (0, i)), pl.BlockSpec((rows, DK), lambda i: (0, i)),
                pl.BlockSpec((rows, DV), lambda i: (0, i)), pl.BlockSpec((KW, DK), lambda i: (0, i)),
                pl.BlockSpec((KW, DK), lambda i: (0, i)), pl.BlockSpec((KW, DV), lambda i: (0, i)),
                self.col, self.row,
            ],
            [
                jax.ShapeDtypeStruct((rows, heads * DK), bf16), jax.ShapeDtypeStruct((rows, heads * DK), bf16),
                jax.ShapeDtypeStruct((rows, heads * DV), bf16), jax.ShapeDtypeStruct((KW, heads * DK), f32),
                jax.ShapeDtypeStruct((KW, heads * DK), f32), jax.ShapeDtypeStruct((KW, heads * DV), f32),
                jax.ShapeDtypeStruct((heads, count, 2), f32), jax.ShapeDtypeStruct((heads, 1, count), f32),
            ],
            "delta_back",
            48,
            [
                pltpu.VMEM((count, DK), f32), pltpu.VMEM((count, DK), f32), pltpu.VMEM((count, DV), f32),
                pltpu.VMEM((PAD + count + 8, DV), f32),
            ],
        )(
            ext, ext, ext, taps, taps, taps, col, row, end, steps, into, inverse, wkey, wval, scores,
            states, fresh, dmixed, query, key,
        )


def rep_piece(block, rows):
    return lax.dynamic_slice_in_dim(block, lax.axis_index("rep") * rows, rows, 0)


def gather_everywhere(block):
    return lax.all_gather(block, ("fsdp", "rep"), axis=0, tiled=True)


def unpacked(parts, gather):
    block = gather(jnp.concatenate(parts, 0))
    block = block.reshape((-1,) + block.shape[-2:])
    whole, at = [], 0
    for part in parts:
        whole.append(block[:, at : at + part.shape[0]].reshape(-1, part.shape[1]))
        at += part.shape[0]
    return whole


def passed_along(block, distance):
    devices = range(lax.axis_size("fsdp"))
    route = [(i - distance, i) for i in devices if i - distance in devices]
    return lax.ppermute(block, "fsdp", route)


def carried_states(transit, offset, backward):
    count = lax.axis_size("fsdp")
    carried = jnp.zeros_like(offset)
    for hop in range(count - 1):
        source = count - 1 - hop if backward else hop
        target = source - 1 if backward else source + 1
        moved = offset
        if hop:
            form = "hed,hef->hdf" if backward else "hde,hef->hdf"
            moved = moved + jnp.einsum(form, transit, carried, preferred_element_type=f32)
        arrived = lax.ppermute(moved.astype(bf16), "fsdp", [(source, target)])
        carried = carried + arrived.astype(f32)
    return carried


def partners(bit):
    return [(i, i ^ bit) for i in range(lax.axis_size("rep"))]


def halves(block, axis, bit):
    mine = (lax.axis_index("rep") // bit) % 2
    return (
        lax.dynamic_index_in_dim(block, mine, axis, keepdims=False),
        lax.dynamic_index_in_dim(block, 1 - mine, axis, keepdims=False),
    )


def halve(block, axis, bit):
    kept, sent = halves(block, axis, bit)
    return kept + lax.ppermute(sent, "rep", partners(bit))


class OwnerSums:
    def __init__(self, grads):
        self.owners, self.reps = lax.axis_size("fsdp"), lax.axis_size("rep")
        self.levels = self.reps.bit_length() - 1
        self.width = grads[0].shape[1]
        self.sizes = [grad.shape[0] // (self.owners * self.reps) for grad in grads]
        cut = (self.owners,) + (2,) * self.levels
        pairs = [
            halves(grad.reshape(cut + (size, self.width)), self.levels, 1)
            for grad, size in zip(grads, self.sizes)
        ]
        kept, sent = [jnp.concatenate(side, -2) for side in zip(*pairs)]
        self.block = kept + lax.ppermute(sent, "rep", partners(1))

    def halve_level(self, level):
        if level == 1:
            self.left = self.block[..., : self.width // 2]
            self.right = self.block[..., self.width // 2 :]
        self.left = halve(self.left, self.levels - level, 1 << level)
        self.right = halve(self.right, 1, 1 << (self.levels - level))

    def scatter(self, *earlier):
        block = jnp.concatenate([self.left, self.right], -1).reshape(-1, self.width)
        for other in earlier:
            block, other.block = lax.optimization_barrier((block, other.block))
        self.block = lax.psum_scatter(block, "fsdp", scatter_dimension=0, tiled=True)


def shared(groups):
    block = lax.all_gather(jnp.concatenate([group.block for group in groups], 0), "rep", axis=0)
    sums, at = [], 0
    for group in groups:
        for size in group.sizes:
            sums.append(block[:, at : at + size].reshape(-1, group.width).astype(f32))
            at += size
    return sums


def sum_everywhere(block):
    for axis in ("rep", "fsdp"):
        size = lax.axis_size(axis)
        bit = 1
        while bit < size:
            block = block + lax.ppermute(block, axis, [(i, i ^ bit) for i in range(size)])
            bit *= 2
    return block


def matmul_low(left, right):
    return jnp.dot(left, right, preferred_element_type=f32)


def matmul_high(left, right):
    return jnp.dot(left, right, precision=highest, preferred_element_type=f32)


def matmul_nt(left, right):
    return lax.dot_general(left, right, (((1,), (1,)), ((), ())), preferred_element_type=f32)


def matmul_tn(left, right):
    return lax.dot_general(left, right, (((0,), (0,)), ((), ())), preferred_element_type=f32)


def rms_scale(values, gain):
    return values * lax.rsqrt(jnp.mean(values * values, -1, keepdims=True) + norm_epsilon) * gain


def swiglu(ff_gate, ff_up):
    return jax.nn.silu(ff_gate) * ff_up


def head_gates(beta_pre, decay_pre, a_log, dt_bias, valid_mask):
    row_count, head_count = beta_pre.shape
    beta_gate = valid_mask * jax.nn.sigmoid(beta_pre)
    log_decay = -valid_mask * jnp.exp(a_log) * jax.nn.softplus(decay_pre + dt_bias)
    cum_log = jnp.cumsum(log_decay.reshape(row_count // CHUNK, CHUNK, head_count), 1)
    return beta_gate, cum_log.reshape(row_count, head_count)


def on_device(
    tokens, cotangent, valid_count, norm_mix, w_query, w_key, w_value, w_gate, w_beta, w_decay,
    a_log, dt_bias, conv_weight, norm_head, w_out, norm_ffn, w_ffgate, w_ffup, w_ffdown,
):
    row_count, width = tokens.shape
    head_count = a_log.shape[0]
    owners, reps = lax.axis_size("fsdp"), lax.axis_size("rep")
    qk_width = head_count * DK
    own_count = valid_count[0, 0]
    valid_mask = (jnp.arange(row_count) < own_count).astype(f32)[:, None]

    share = w_query.shape[0] // reps
    w_qkv = gather_everywhere(
        jnp.concatenate([rep_piece(w, share) for w in (w_query, w_key, w_value)], 1)
    )
    gate_pieces = rep_piece(w_gate, share)
    gate_left, gate_right, out_full, ffgate_t, ffup_t, ffdown_full = unpacked(
        [
            gate_pieces[:, :width],
            gate_pieces[:, width:],
            rep_piece(w_out, w_out.shape[0] // reps),
            rep_piece(w_ffgate.T, w_ffgate.shape[1] // reps),
            rep_piece(w_ffup.T, w_ffup.shape[1] // reps),
            rep_piece(w_ffdown, w_ffdown.shape[0] // reps),
        ],
        lambda block: lax.all_gather(
            lax.optimization_barrier((block, w_qkv))[0], ("fsdp", "rep")
        ),
    )

    small = [norm_mix, norm_ffn, norm_head, w_beta.reshape(-1), w_decay.reshape(-1), conv_weight.reshape(-1)]
    small_full = lax.all_gather(jnp.concatenate(small), "fsdp", axis=0)
    at, pieces = 0, []
    for part in small:
        pieces.append(small_full[:, at : at + part.shape[0]])
        at += part.shape[0]
    mix_gain, ffn_gain, head_gain = [p.reshape(-1).astype(f32) for p in pieces[:3]]
    w_beta_decay = jnp.concatenate([p.reshape(width, head_count) for p in pieces[3:5]], 1)
    taps = pieces[5].reshape(owners, KW, -1).transpose(1, 0, 2).reshape(KW, -1).astype(f32)
    head_gain = head_gain[None, :]

    inputs = tokens.astype(f32)
    edge_place = own_count - (KW - 1)
    before = passed_along(lax.dynamic_slice_in_dim(tokens, edge_place, KW - 1, 0), 1)
    ahead = jnp.concatenate([jnp.zeros((PAD - KW + 1, width), f32), before.astype(f32)], 0)
    normed_f32, mix_pull = jax.vjp(rms_scale, inputs, mix_gain)
    normed = normed_f32.astype(bf16)
    normed_ext = jnp.concatenate([rms_scale(ahead, mix_gain).astype(bf16), normed], 0)
    normed_ext, taps, w_qkv = lax.optimization_barrier((normed_ext, taps, w_qkv))
    projected = matmul_low(normed_ext, w_qkv)
    gates_pre = matmul_low(normed, w_beta_decay)
    beta_pre, decay_pre = gates_pre[:, :head_count], gates_pre[:, head_count:]
    (beta_gate, cum_log), gates_pull = jax.vjp(
        lambda *args: head_gates(*args, valid_mask), beta_pre, decay_pre, a_log, dt_bias
    )
    col = jnp.stack([beta_gate.T, cum_log.T], -1)
    row = cum_log.T[:, None, :]
    calls = HeadCalls(row_count, head_count)
    query, key, inverse, wkey, wval, scores, steps, maps, end_map = calls.front(projected, taps, col, row)
    transit = end_map[:, :, :DK]
    start_state = carried_states(transit, end_map[:, :, DK:], False)
    gate_pre = jnp.concatenate([matmul_low(normed, gate_left), matmul_low(normed, gate_right)], 1)
    mixed, states, fresh, gated_out = calls.outputs(
        query, maps, start_state, wkey, wval, scores, col, gate_pre, head_gain
    )
    residual = inputs + matmul_low(gated_out, out_full)

    ffn_f32, ffn_pull = jax.vjp(rms_scale, residual, ffn_gain)
    normed_ffn = ffn_f32.astype(bf16)
    swiglu_f32, swiglu_pull = jax.vjp(
        swiglu, matmul_nt(normed_ffn, ffgate_t), matmul_nt(normed_ffn, ffup_t)
    )
    swiglu_out = swiglu_f32.astype(bf16)
    output = (valid_mask * (residual + matmul_low(swiglu_out, ffdown_full))).astype(bf16)
    out_grad = cotangent.astype(f32) * valid_mask
    out_low = out_grad.astype(bf16)
    gate_grad_f32, up_grad_f32 = swiglu_pull(matmul_nt(out_low, ffdown_full))
    gate_low = gate_grad_f32.astype(bf16)
    up_low = up_grad_f32.astype(bf16)
    ffn_in_grad = matmul_low(gate_low, ffgate_t) + matmul_low(up_low, ffup_t)
    residual_part, ffn_gain_grad = ffn_pull(ffn_in_grad)
    residual_grad = out_grad + residual_part
    residual_low = residual_grad.astype(bf16)

    dgated = matmul_nt(residual_low, out_full)
    dgate_low, dmixed, into, own_grad, dgain = calls.tail_back(
        dgated, mixed, gate_pre, head_gain, query, scores, wkey, steps, col
    )
    end_grad = carried_states(transit, own_grad, True)

    ffn_sums = OwnerSums([
        matmul_tn(swiglu_out, out_low).astype(bf16),
        matmul_tn(gate_low, normed_ffn).astype(bf16),
        matmul_tn(up_low, normed_ffn).astype(bf16),
    ])
    ffn_sums.halve_level(1)
    mixer_sums = OwnerSums([
        matmul_tn(gated_out, residual_low).astype(bf16),
        matmul_tn(normed, dgate_low[:, :width]).astype(bf16),
        matmul_tn(normed, dgate_low[:, width:]).astype(bf16),
    ])
    end_grad, ffn_sums.left, ffn_sums.right, mixer_sums.block = lax.optimization_barrier(
        (end_grad, ffn_sums.left, ffn_sums.right, mixer_sums.block)
    )
    for level in range(2, ffn_sums.levels):
        ffn_sums.halve_level(level)
    mixer_sums.halve_level(1)

    dxq, dxk, dxv, dtap_q, dtap_k, dtap_v, dcol, drow = calls.back(
        projected, taps, col, row, end_grad, steps, into, inverse, wkey, wval, scores, states, fresh,
        dmixed, query, key,
    )
    dprojected = jnp.concatenate([dxq, dxk, dxv], 1)
    column_blocks = [dprojected[:, at : at + width] for at in range(0, dprojected.shape[1], width)]
    qkv_sums = OwnerSums([matmul_tn(normed_ext, block).astype(bf16) for block in column_blocks])
    qkv_sums.halve_level(1)
    coming = passed_along(dprojected[PAD - KW + 1 : PAD], -1)
    own_low = dprojected[PAD:]
    edge_rows = lax.dynamic_slice_in_dim(own_low, edge_place, KW - 1, 0).astype(f32) + coming.astype(f32)
    own_low = lax.dynamic_update_slice_in_dim(own_low, edge_rows.astype(bf16), edge_place, 0)
    beta_pre_grad, decay_pre_grad, rate_grad, bias_grad = gates_pull(
        (dcol[:, :, 0].T, (dcol[:, :, 1] + drow[:, 0, :]).T)
    )
    gates_grad = jnp.concatenate([beta_pre_grad, decay_pre_grad], 1)
    normed_grad = (
        matmul_nt(own_low, w_qkv)
        + matmul_nt(dgate_low[:, :width], gate_left)
        + matmul_nt(dgate_low[:, width:], gate_right)
        + matmul_high(gates_grad, w_beta_decay.astype(f32).T)
    )
    gates_weight_grad = lax.dot_general(
        normed.astype(f32), gates_grad, (((0,), (0,)), ((), ())), precision=highest,
        preferred_element_type=f32,
    )
    qkv_sums.left, qkv_sums.right, normed_grad, gates_weight_grad = lax.optimization_barrier(
        (qkv_sums.left, qkv_sums.right, normed_grad, gates_weight_grad)
    )
    ffn_sums.scatter()
    for level in range(2, mixer_sums.levels):
        mixer_sums.halve_level(level)
    mixer_sums.scatter(ffn_sums)
    for level in range(2, qkv_sums.levels):
        qkv_sums.halve_level(level)
    qkv_sums.scatter(mixer_sums)
    (
        ffdown_grad, ffgate_grad, ffup_grad, out_weight_grad, gate_left_grad, gate_right_grad, *qkv_grads
    ) = shared([ffn_sums, mixer_sums, qkv_sums])
    qkv_grad = jnp.concatenate(qkv_grads, 1)
    input_part, mix_gain_grad = mix_pull(normed_grad)
    grad_tokens = residual_grad + input_part

    dtaps = jnp.concatenate([dtap_q, dtap_k, dtap_v], 1)
    small = [
        mix_gain_grad, ffn_gain_grad, jnp.sum(dgain, 0).reshape(-1), gates_weight_grad.reshape(-1),
        dtaps.reshape(-1), rate_grad, bias_grad,
    ]
    flat = jnp.concatenate(small)
    lanes = 128
    flat = jnp.pad(flat, (0, -flat.shape[0] % (8 * lanes))).reshape(-1, lanes)
    sums = sum_everywhere(flat).reshape(-1)
    at, pieces = 0, []
    for part in small:
        pieces.append(sums[at : at + part.shape[0]])
        at += part.shape[0]
    mine = lax.axis_index("fsdp")

    def own(block, axis):
        size = block.shape[axis] // owners
        return lax.dynamic_slice_in_dim(block, mine * size, size, axis)

    gates_weight = own(pieces[3].reshape(width, 2 * head_count), 0)
    return (
        output,
        grad_tokens,
        own(pieces[0], 0),
        qkv_grad[:, :qk_width],
        qkv_grad[:, qk_width : 2 * qk_width],
        qkv_grad[:, 2 * qk_width :],
        jnp.concatenate([gate_left_grad, gate_right_grad], 1),
        gates_weight[:, :head_count],
        gates_weight[:, head_count:],
        pieces[5],
        pieces[6],
        own(pieces[4].reshape(KW, -1), 1),
        own(pieces[2], 0),
        out_weight_grad,
        own(pieces[1], 0),
        ffgate_grad.T,
        ffup_grad.T,
        ffdown_grad,
    )


def solution(mesh):
    rows = P(("rep", "fsdp"), None)
    first, second, vector = P("fsdp", None), P(None, "fsdp"), P("fsdp")
    placed = (
        rows, rows, P("rep", "fsdp"), vector, first, first, first, first, first, first, P(), P(),
        second, vector, first, vector, second, second, first,
    )
    given = (
        rows, rows, vector, first, first, first, first, first, first, P(), P(), second, vector, first,
        vector, second, second, first,
    )
    return jax.shard_map(on_device, mesh=mesh, in_specs=placed, out_specs=given, check_vma=False)
```
